32 devices in a mesh: groups: 2 (over y), serve: 4 (over x, core), tensor: 4 (over z).
Axes of the slice: x: 2, y: 2, z: 4, core: 2. Of those that a mesh axis runs over, the one named last changes fastest.
Arguments:
- tokens: bfloat16 [4096, 8192], P(('groups', 'serve'), 'tensor'), parts along dimension 0, may hold values from -6 to 6
- base_weight: bfloat16 [8192, 4096], P('tensor'), may hold values from -0.09375 to 0.09375
- adapter_down: bfloat16 [8, 64, 8192], P('serve', None, 'tensor'), may hold values from -0.0625 to 0.0625
- adapter_up: bfloat16 [8, 64, 4096], P('serve', None, 'tensor'), may hold values from -0.75 to 0.75
- segment_adapter: int32 [16], P('groups'), parts along dimension 0, may hold values from 0 to 7
- owner_map: int32 [16], P('groups'), parts along dimension 0, may hold values from 0 to 7, as said below
- segment_blocks: int32 [16], P(('groups', 'serve')), parts along dimension 0, may hold values from 1 to 2
Outputs:
- mixed: bfloat16 [4096, 4096], P(('groups', 'serve'), 'tensor'), parts along dimension 0
The draws below stay inside these ranges and needn't reach their ends.
There are 2 independent parts, one for each index of `groups`. The reference program is written for one: setup_inputs(seed, part) draws one part's arguments, and reference() takes and returns one part's arrays. A program takes and returns all parts, laid end to end along the dimension named above; an argument that names none is the same for every part. Nothing has to cross between parts.
Inputs may be any that keep to these rules, and one draw needn't show every extreme that they name: owner_map is a permutation of the store rows; the adapters named by the segments of one serve device lie in store rows of pairwise different serve devices (row // 2).
All inputs are finite; a program needn't handle non-finite values.
Results may differ from the reference program's by a relative error of at most 0.012.
Values may be sent and summed in bfloat16 or wider, within the bound.
A program may use at most 128 MiB of HBM per device.

```python
import jax
import jax.numpy as jnp
from jax import lax

D = 8192
OUTPUT_FEATURES = 4096
R = 64
AD_DEV = 2
SEG_DEV = 2
BLOCK = 128
SEGMENT_LENGTH = 256
MATCH_SEGMENTS = 8
ADAPTERS = 8
TOKENS = 2048
N_SERVE = 4
N_TENSOR = 4


def segment_plan(key):
    owner_key, slot_key, first_key, offset_key, turn_key = jax.random.split(key, 5)
    storage = jax.random.permutation(owner_key, ADAPTERS).astype(jnp.int32)
    rotation = jax.random.randint(turn_key, (), 0, N_SERVE)
    first_owner = jnp.min(jax.random.randint(first_key, (N_SERVE, 3), 0, N_SERVE), axis=1)
    first_owner = (first_owner + rotation) % N_SERVE
    others = jax.vmap(lambda single: jax.random.permutation(single, N_SERVE - 1))(jax.random.split(offset_key, N_SERVE))
    offsets = jnp.concatenate([jnp.zeros((N_SERVE, 1), jnp.int32), others[:, :SEG_DEV - 1].astype(jnp.int32) + 1], axis=1)
    owners = (first_owner[:, None] + offsets) % N_SERVE
    slot_within = jax.random.randint(slot_key, (N_SERVE, SEG_DEV), 0, AD_DEV)
    store_rows = (owners * AD_DEV + slot_within).reshape(-1).astype(jnp.int32)
    inverse = jnp.zeros((ADAPTERS,), jnp.int32).at[storage].set(jnp.arange(ADAPTERS, dtype=jnp.int32))
    return (storage, inverse[store_rows])


def draw_owner_map(key, part):
    return segment_plan(key)[0]


def draw_segment_adapter(key, part):
    return segment_plan(key)[1]


def place_ends(values, rng, least, largest):
    longest = values.shape.index(max(values.shape))
    spots = []
    for shift in (0, 1):
        where = [jax.random.randint(jax.random.fold_in(rng, axis), (), 0, length) for axis, length in enumerate(values.shape)]
        where[longest] = (where[longest] + shift) % values.shape[longest]
        spots.append(tuple(where))
    return values.at[spots[0]].set(least).at[spots[1]].set(largest)


def spiked(values, key, source, target, shards_of, factor):
    def block_of(dim):
        return (jnp.arange(values.shape[dim]) // (values.shape[dim] // shards_of)).reshape((-1,) + (1,) * (values.ndim - 1 - dim))

    one_side = jax.random.permutation(key, shards_of)[block_of(target)]
    second = (block_of(target) + shards_of // 2) % shards_of
    return jnp.where((block_of(source) == one_side) | (block_of(source) == second), factor * values, values)


def level_of(rng, dims, pieces, least, top_value):
    def one(dim, blocks):
        steps = jax.random.uniform(jax.random.fold_in(jax.random.fold_in(rng, 6), dim), (blocks,), jnp.float32, least / len(pieces), top_value / len(pieces))
        return jnp.repeat(jnp.exp(steps), dims[dim] // blocks).reshape((-1,) + (1,) * (len(dims) - dim - 1))

    gain = one(*pieces[0])
    for cut in pieces[1:]:
        gain = gain * one(*cut)
    return gain


def bell_draw(own_key, extent, spread, bound, shards=(), kind=jnp.bfloat16):
    drawn = jax.random.normal(own_key, extent, jnp.float32) * spread
    if len(shards) > 0:
        drawn = level_of(own_key, extent, shards, -0.22, 0.18) * drawn
    return jnp.clip(drawn, min=-bound, max=bound).astype(kind)


def bell_draw_with(key, extent, width, limit, cuts, heavy, held_as=jnp.bfloat16):
    drawn = width * jax.random.normal(key, extent, jnp.float32)
    if cuts:
        drawn = drawn * level_of(key, extent, cuts, -0.22, 0.18)
    return jnp.clip(spiked(drawn, jax.random.fold_in(key, 3), *heavy), -limit, limit).astype(held_as)


def setup_inputs(seed: int = 0, part: int = 0) -> dict:
    arg_keys = jax.random.split(jax.random.key(seed), 8)
    part_keys = jax.random.split(jax.random.fold_in(arg_keys[7], part), 8)
    return {
        "tokens": bell_draw(part_keys[0], (TOKENS, D), 1.0, 6.0, ((0, 4), (1, 4))),
        "base_weight": bell_draw_with(arg_keys[1], (D, OUTPUT_FEATURES), D ** -0.5, 0.09375, ((0, 4),), (0, 1, 4, 2.0)),
        "adapter_down": bell_draw(arg_keys[2], (ADAPTERS, R, D), D ** -0.5, 0.0625, ((0, 4), (2, 4))),
        "adapter_up": bell_draw(arg_keys[3], (ADAPTERS, R, OUTPUT_FEATURES), R ** -0.5, 0.75, ((0, 4), (2, 4))),
        "segment_adapter": draw_segment_adapter(jax.random.fold_in(jax.random.fold_in(arg_keys[7], part), 71), part),
        "owner_map": draw_owner_map(jax.random.fold_in(jax.random.fold_in(arg_keys[7], part), 71), part),
        "segment_blocks": place_ends(jax.random.randint(part_keys[6], (MATCH_SEGMENTS,), 1, 3), jax.random.fold_in(part_keys[6], 1), 1, 2).astype(jnp.int32),
    }


low_rank_scale = 0.5


def reference(tokens, base_weight, adapter_down, adapter_up, segment_adapter, owner_map, segment_blocks):
    shard_width = D // N_TENSOR
    frozen_sum = jnp.zeros((TOKENS, OUTPUT_FEATURES), jnp.float32)
    for column_group in range(N_TENSOR):
        lower = column_group * shard_width
        partial_value = jnp.dot(tokens[:, lower:lower + shard_width], base_weight[lower:lower + shard_width, :], preferred_element_type=jnp.float32)
        frozen_sum = frozen_sum + lax.optimization_barrier(partial_value.astype(jnp.bfloat16)).astype(jnp.float32)
    store_row = owner_map[segment_adapter].astype(jnp.int32)
    down_rows = adapter_down[store_row].astype(jnp.float32)
    expand_rows = adapter_up[store_row].astype(jnp.float32)
    token_segments = tokens.reshape(MATCH_SEGMENTS, SEGMENT_LENGTH, D).astype(jnp.float32)
    rank_reduce = jnp.einsum("ctd,crd->ctr", token_segments, down_rows, precision=lax.Precision.HIGHEST).astype(jnp.bfloat16)
    low_rank_delta = jnp.einsum("spi,sij->spj", rank_reduce.astype(jnp.float32), expand_rows, precision=lax.Precision.HIGHEST)
    active_rows = jnp.arange(SEGMENT_LENGTH, dtype=jnp.int32)[None, :] < segment_blocks[:, None] * BLOCK
    mixed = jnp.where(active_rows[:, :, None], frozen_sum.reshape(MATCH_SEGMENTS, SEGMENT_LENGTH, OUTPUT_FEATURES) + low_rank_scale * low_rank_delta, 0.0)
    return mixed.reshape(TOKENS, OUTPUT_FEATURES).astype(jnp.bfloat16)
```

```python
import functools

import jax
import jax.numpy as jnp
from jax import lax
from jax.experimental import pallas as pl
from jax.experimental.pallas import tpu as pltpu
from jax.sharding import PartitionSpec as P

MESH = pl.DeviceIdType.MESH
BLOCK = 128
WIDTH = 256
AHEAD = 3

low_rank_scale = 0.5


def kernel(
    n,
    n_serve,
    seg_adapter,
    owner_map,
    tok_hbm,
    w_hbm,
    down_hbm,
    up_hbm,
    out_hbm,
    tok,
    w,
    acc,
    send,
    from_left,
    from_right,
    own,
    out,
    down,
    up,
    down_send,
    up_send,
    down_got,
    up_got,
    rank_own,
    rank_send,
    rank_got,
    local_sem,
    w_sem,
    out_sem,
    send_sem,
    left_sem,
    right_sem,
    down_ssem,
    down_rsem,
    up_ssem,
    up_rsem,
    rank_ssem,
    rank_rsem,
):
    z = lax.axis_index("tensor")
    me = lax.axis_index("serve")
    chunks = w.shape[0]
    per = chunks // n
    steps = chunks - per
    stored, rank = down.shape[0], down.shape[1]
    rows = tok.shape[0]
    segs = seg_adapter.shape[0] // n_serve
    seg_len = rows // segs
    first_right = (z + 1) * per
    first_own = z * per

    def load_w(q):
        return pltpu.make_async_copy(
            w_hbm.at[:, pl.ds(pl.multiple_of(q * WIDTH, WIDTH), WIDTH)], w.at[q], w_sem.at[q]
        )

    load_tok = pltpu.make_async_copy(tok_hbm, tok, local_sem.at[0])
    load_down = pltpu.make_async_copy(down_hbm, down, local_sem.at[1])
    load_up = pltpu.make_async_copy(up_hbm, up, local_sem.at[2])

    barrier = pltpu.get_barrier_semaphore()

    @pl.loop(1, n_serve)
    def _(k):
        pl.semaphore_signal(
            barrier, inc=1, device_id={"serve": lax.rem(me + k, n_serve)}, device_id_type=MESH
        )

    @pl.when(z > 0)
    def _():
        pl.semaphore_signal(barrier, inc=1, device_id={"tensor": z - 1}, device_id_type=MESH)

    @pl.when(z < n - 1)
    def _():
        pl.semaphore_signal(barrier, inc=1, device_id={"tensor": z + 1}, device_id_type=MESH)

    load_tok.start()

    def load_step(i):
        @pl.when(chunks - 1 - i >= first_right)
        def _():
            load_w(chunks - 1 - i).start()

        @pl.when(i < first_own)
        def _():
            load_w(i).start()

    load_step(0)
    load_down.start()
    load_up.start()

    @pl.loop(1, steps)
    def _(i):
        load_step(i)

    @pl.loop(0, per)
    def _(c):
        load_w(first_own + c).start()

    def row_for(peer):
        row = jnp.int32(0)
        for j in range(segs):
            stored_row = owner_map[seg_adapter[peer * segs + j]]
            row += jnp.where(lax.div(stored_row, stored) == me, lax.rem(stored_row, stored), 0)
        return row

    def owner_of(j):
        return lax.div(owner_map[seg_adapter[me * segs + j]], stored)

    def adapter_copy(k, src, dst, ssem, rsem):
        peer = lax.rem(me + k, n_serve)
        return pltpu.make_async_remote_copy(
            src_ref=src.at[peer],
            dst_ref=dst.at[me],
            send_sem=ssem.at[peer],
            recv_sem=rsem.at[me],
            device_id={"serve": peer},
            device_id_type=MESH,
        )

    def adapter_wait(k, src, dst, ssem, rsem):
        peer = lax.rem(me + k, n_serve)
        got = pltpu.make_async_remote_copy(
            src_ref=src.at[peer],
            dst_ref=dst.at[peer],
            send_sem=ssem.at[peer],
            recv_sem=rsem.at[peer],
            device_id={"serve": peer},
            device_id_type=MESH,
        )
        got.wait_send()
        got.wait_recv()

    load_down.wait()
    neighbours = (z > 0).astype(jnp.int32) + (z < n - 1).astype(jnp.int32)
    pl.semaphore_wait(barrier, n_serve - 1 + neighbours)

    @pl.loop(1, n_serve)
    def _(k):
        peer = lax.rem(me + k, n_serve)
        down_send[peer] = down[row_for(peer)]
        adapter_copy(k, down_send, down_got, down_ssem, down_rsem).start()

    down_got[me] = down[row_for(me)]
    load_tok.wait()

    def chunk_copy(q, to_right):
        return pltpu.make_async_remote_copy(
            src_ref=send.at[q],
            dst_ref=(from_left if to_right else from_right).at[q],
            send_sem=send_sem.at[q],
            recv_sem=(left_sem if to_right else right_sem).at[q],
            device_id={"tensor": z + 1 if to_right else z - 1},
            device_id_type=MESH,
        )

    def rank_copy(to_right):
        side = 0 if to_right else 1
        return pltpu.make_async_remote_copy(
            src_ref=rank_send.at[side],
            dst_ref=rank_got.at[side],
            send_sem=rank_ssem.at[side],
            recv_sem=rank_rsem.at[side],
            device_id={"tensor": z + 1 if to_right else z - 1},
            device_id_type=MESH,
        )

    def base_step(i, q, to_right):
        load_w(q).wait()
        acc[...] = jnp.dot(tok[...], w[q], preferred_element_type=jnp.float32)
        behind = (z > 0) if to_right else (z < n - 1)

        @pl.when(behind)
        def _():
            chunk_copy(q, to_right).wait_recv()
            got = (from_left if to_right else from_right)[q]
            send[q] = (acc[...] + got.astype(jnp.float32)).astype(jnp.bfloat16)

        @pl.when(jnp.logical_not(behind))
        def _():
            send[q] = acc[...].astype(jnp.bfloat16)

        @pl.when(i >= AHEAD)
        def _():
            chunk_copy(q + AHEAD if to_right else q - AHEAD, to_right).wait_send()

        chunk_copy(q, to_right).start()

    def base_steps(i):
        @pl.when(chunks - 1 - i >= first_right)
        def _():
            base_step(i, chunks - 1 - i, True)

        @pl.when(i < first_own)
        def _():
            base_step(i, i, False)

    def rank_steps():
        @pl.loop(1, n_serve)
        def _(k):
            adapter_wait(k, down_send, down_got, down_ssem, down_rsem)

        for j in range(segs):
            at = pl.ds(j * seg_len, seg_len)
            rank_own[:, at] = lax.dot_general(
                down_got[owner_of(j)],
                tok[at, :],
                (((1,), (1,)), ((), ())),
                preferred_element_type=jnp.float32,
            )
        for to_right in (True, False):
            side = 0 if to_right else 1
            behind = (z > 0) if to_right else (z < n - 1)
            ahead = (z < n - 1) if to_right else (z > 0)

            @pl.when(behind)
            def _():
                rank_copy(to_right).wait_recv()

                @pl.when(ahead)
                def _():
                    rank_send[side] = (
                        rank_own[...] + rank_got[side].astype(jnp.float32)
                    ).astype(jnp.bfloat16)

            @pl.when(jnp.logical_not(behind))
            def _():
                rank_got[side] = jnp.zeros(rank_got.shape[1:], rank_got.dtype)

                @pl.when(ahead)
                def _():
                    rank_send[side] = rank_own[...].astype(jnp.bfloat16)

            @pl.when(ahead)
            def _():
                rank_copy(to_right).start()

    middle = min(6, steps - 1)

    @pl.loop(0, 2)
    def _(i):
        base_steps(i)

    load_up.wait()

    @pl.loop(1, n_serve)
    def _(k):
        peer = lax.rem(me + k, n_serve)
        up_send[peer] = up[row_for(peer)]
        adapter_copy(k, up_send, up_got, up_ssem, up_rsem).start()

    up_got[me] = up[row_for(me)]

    @pl.loop(2, steps)
    def _(i):
        base_steps(i)

        @pl.when(i == middle)
        def _():
            rank_steps()

    @pl.loop(1, n_serve)
    def _(k):
        adapter_wait(k, up_send, up_got, up_ssem, up_rsem)

    coords = (
        rank_own[...] + rank_got[0].astype(jnp.float32) + rank_got[1].astype(jnp.float32)
    ).astype(jnp.bfloat16)
    for c in range(per):
        load_w(first_own + c).wait()
        own[c] = jnp.dot(tok[...], w[first_own + c], preferred_element_type=jnp.float32)
        for j in range(segs):
            at = pl.ds(j * seg_len, seg_len)
            own[c, at, :] += low_rank_scale * lax.dot_general(
                coords[:, j * seg_len : (j + 1) * seg_len],
                up_got[owner_of(j), :, c * WIDTH : (c + 1) * WIDTH],
                (((0,), (0,)), ((), ())),
                preferred_element_type=jnp.float32,
            )

    def out_copy(c):
        return pltpu.make_async_copy(
            out.at[c], out_hbm.at[:, pl.ds(pl.multiple_of(c * WIDTH, WIDTH), WIDTH)], out_sem.at[c]
        )

    @pl.loop(0, per)
    def _(k):
        c = jnp.where(2 * z < n, per - 1 - k, k)
        q = first_own + c

        @pl.when(z > 0)
        def _():
            chunk_copy(q, True).wait_recv()
            own[c] += from_left[q].astype(jnp.float32)

        @pl.when(z < n - 1)
        def _():
            chunk_copy(q, False).wait_recv()
            own[c] += from_right[q].astype(jnp.float32)

        out[c] = own[c].astype(jnp.bfloat16)
        out_copy(c).start()

    @pl.loop(0, per)
    def _(c):
        out_copy(c).wait()

    @pl.loop(0, steps)
    def _(i):
        @pl.when((chunks - 1 - i >= first_right) & (chunks - 1 - i - AHEAD < first_right))
        def _():
            chunk_copy(chunks - 1 - i, True).wait_send()

        @pl.when((i < first_own) & (i + AHEAD >= first_own))
        def _():
            chunk_copy(i, False).wait_send()

    @pl.when(z < n - 1)
    def _():
        rank_copy(True).wait_send()

    @pl.when(z > 0)
    def _():
        rank_copy(False).wait_send()


def on_device(
    n,
    n_serve,
    tokens,
    base_weight,
    adapter_down,
    adapter_up,
    segment_adapter,
    owner_map,
    segment_blocks,
):
    rows, depth = tokens.shape
    columns = base_weight.shape[1]
    chunks = columns // WIDTH
    out_width = columns // n
    per = out_width // WIDTH
    stored, rank, _ = adapter_down.shape
    bf16, f32 = jnp.bfloat16, jnp.float32
    smem = pl.BlockSpec(memory_space=pltpu.SMEM)
    anywhere = pl.BlockSpec(memory_space=pl.ANY)
    dma = pltpu.SemaphoreType.DMA
    summed = pl.pallas_call(
        functools.partial(kernel, n, n_serve),
        out_shape=jax.ShapeDtypeStruct((rows, out_width), bf16),
        in_specs=[smem, smem, anywhere, anywhere, anywhere, anywhere],
        out_specs=anywhere,
        scratch_shapes=[
            pltpu.VMEM((rows, depth), bf16),
            pltpu.VMEM((chunks, depth, WIDTH), bf16),
            pltpu.VMEM((rows, WIDTH), f32),
            pltpu.VMEM((chunks, rows, WIDTH), bf16),
            pltpu.VMEM((chunks, rows, WIDTH), bf16),
            pltpu.VMEM((chunks, rows, WIDTH), bf16),
            pltpu.VMEM((per, rows, WIDTH), f32),
            pltpu.VMEM((per, rows, WIDTH), bf16),
            pltpu.VMEM((stored, rank, depth), bf16),
            pltpu.VMEM((stored, rank, out_width), bf16),
            pltpu.VMEM((n_serve, rank, depth), bf16),
            pltpu.VMEM((n_serve, rank, out_width), bf16),
            pltpu.VMEM((n_serve, rank, depth), bf16),
            pltpu.VMEM((n_serve, rank, out_width), bf16),
            pltpu.VMEM((rank, rows), f32),
            pltpu.VMEM((2, rank, rows), bf16),
            pltpu.VMEM((2, rank, rows), bf16),
            dma((3,)),
            dma((chunks,)),
            dma((per,)),
            dma((chunks,)),
            dma((chunks,)),
            dma((chunks,)),
            dma((n_serve,)),
            dma((n_serve,)),
            dma((n_serve,)),
            dma((n_serve,)),
            dma((2,)),
            dma((2,)),
        ],
        compiler_params=pltpu.CompilerParams(
            collective_id=0, has_side_effects=True, vmem_limit_bytes=56 * 2**20
        ),
        cost_estimate=pl.CostEstimate(
            flops=2 * rows * depth * columns,
            bytes_accessed=2 * (depth * columns + rows * depth + rows * out_width),
            transcendentals=0,
        ),
    )(segment_adapter, owner_map, tokens, base_weight, adapter_down, adapter_up)
    segments = segment_blocks.shape[0]
    live = jnp.arange(rows // segments, dtype=jnp.int32)[None, :] < segment_blocks[:, None] * BLOCK
    return jnp.where(live.reshape(-1)[:, None], summed, jnp.zeros((), bf16))


def solution(mesh):
    in_specs = (
        P(("groups", "serve"), "tensor"),
        P("tensor", None),
        P("serve", None, "tensor"),
        P("serve", None, "tensor"),
        P("groups"),
        P("groups"),
        P(("groups", "serve")),
    )
    out_specs = P(("groups", "serve"), "tensor")
    return jax.shard_map(
        functools.partial(on_device, mesh.shape["tensor"], mesh.shape["serve"]),
        mesh=mesh,
        in_specs=in_specs,
        out_specs=out_specs,
        check_vma=False,
    )
```

```python
import functools

import jax
import jax.numpy as jnp
from jax import lax
from jax.experimental import pallas as pl
from jax.experimental.pallas import tpu as pltpu
from jax.sharding import PartitionSpec as P

MESH = pl.DeviceIdType.MESH
BLOCK = 128
WIDTH = 256
RANK_STEP = 3
RANK_LAG = 4
AHEAD = 3

low_rank_scale = 0.5


def kernel(
    n,
    n_serve,
    seg_adapter,
    owner_map,
    tok_hbm,
    w_hbm,
    down_hbm,
    up_hbm,
    out_hbm,
    tok,
    w,
    acc,
    send,
    from_left,
    from_right,
    own,
    out,
    down,
    up,
    down_send,
    up_send,
    down_got,
    up_got,
    rank_own,
    rank_send,
    rank_got,
    local_sem,
    w_sem,
    out_sem,
    send_sem,
    left_sem,
    right_sem,
    down_ssem,
    down_rsem,
    up_ssem,
    up_rsem,
    rank_ssem,
    rank_rsem,
):
    z = lax.axis_index("tensor")
    me = lax.axis_index("serve")
    chunks = w.shape[0]
    per = chunks // n
    steps = chunks - per
    stored, rank = down.shape[0], down.shape[1]
    rows = tok.shape[0]
    segs = seg_adapter.shape[0] // n_serve
    seg_len = rows // segs
    first_right = (z + 1) * per
    first_own = z * per

    def load_w(q):
        return pltpu.make_async_copy(
            w_hbm.at[:, pl.ds(pl.multiple_of(q * WIDTH, WIDTH), WIDTH)], w.at[q], w_sem.at[q]
        )

    load_tok = pltpu.make_async_copy(tok_hbm, tok, local_sem.at[0])
    load_down = pltpu.make_async_copy(down_hbm, down, local_sem.at[1])
    load_up = pltpu.make_async_copy(up_hbm, up, local_sem.at[2])

    barrier = pltpu.get_barrier_semaphore()

    @pl.loop(1, n_serve)
    def _(k):
        pl.semaphore_signal(
            barrier, inc=1, device_id={"serve": lax.rem(me + k, n_serve)}, device_id_type=MESH
        )

    @pl.when(z > 0)
    def _():
        pl.semaphore_signal(barrier, inc=1, device_id={"tensor": z - 1}, device_id_type=MESH)

    @pl.when(z < n - 1)
    def _():
        pl.semaphore_signal(barrier, inc=1, device_id={"tensor": z + 1}, device_id_type=MESH)

    load_tok.start()

    def load_step(i):
        @pl.when(chunks - 1 - i >= first_right)
        def _():
            load_w(chunks - 1 - i).start()

        @pl.when(i < first_own)
        def _():
            load_w(i).start()

    load_step(0)
    load_down.start()
    load_up.start()

    @pl.loop(1, steps)
    def _(i):
        load_step(i)

    @pl.loop(0, per)
    def _(c):
        load_w(first_own + c).start()

    def row_for(peer):
        row = jnp.int32(0)
        for j in range(segs):
            stored_row = owner_map[seg_adapter[peer * segs + j]]
            row += jnp.where(lax.div(stored_row, stored) == me, lax.rem(stored_row, stored), 0)
        return row

    def owner_of(j):
        return lax.div(owner_map[seg_adapter[me * segs + j]], stored)

    def adapter_copy(k, src, dst, ssem, rsem):
        peer = lax.rem(me + k, n_serve)
        return pltpu.make_async_remote_copy(
            src_ref=src.at[peer],
            dst_ref=dst.at[me],
            send_sem=ssem.at[peer],
            recv_sem=rsem.at[me],
            device_id={"serve": peer},
            device_id_type=MESH,
        )

    def adapter_wait(k, src, dst, ssem, rsem):
        peer = lax.rem(me + k, n_serve)
        got = pltpu.make_async_remote_copy(
            src_ref=src.at[peer],
            dst_ref=dst.at[peer],
            send_sem=ssem.at[peer],
            recv_sem=rsem.at[peer],
            device_id={"serve": peer},
            device_id_type=MESH,
        )
        got.wait_send()
        got.wait_recv()

    load_down.wait()
    neighbours = (z > 0).astype(jnp.int32) + (z < n - 1).astype(jnp.int32)
    pl.semaphore_wait(barrier, n_serve - 1 + neighbours)

    @pl.loop(1, n_serve)
    def _(k):
        peer = lax.rem(me + k, n_serve)
        down_send[peer] = down[row_for(peer)]
        adapter_copy(k, down_send, down_got, down_ssem, down_rsem).start()

    down_got[me] = down[row_for(me)]
    load_tok.wait()

    def chunk_copy(q, to_right):
        return pltpu.make_async_remote_copy(
            src_ref=send.at[q],
            dst_ref=(from_left if to_right else from_right).at[q],
            send_sem=send_sem.at[q],
            recv_sem=(left_sem if to_right else right_sem).at[q],
            device_id={"tensor": z + 1 if to_right else z - 1},
            device_id_type=MESH,
        )

    def rank_copy(to_right):
        side = 0 if to_right else 1
        return pltpu.make_async_remote_copy(
            src_ref=rank_send.at[side],
            dst_ref=rank_got.at[side],
            send_sem=rank_ssem.at[side],
            recv_sem=rank_rsem.at[side],
            device_id={"tensor": z + 1 if to_right else z - 1},
            device_id_type=MESH,
        )

    def base_step(i, q, to_right):
        load_w(q).wait()
        acc[...] = jnp.dot(tok[...], w[q], preferred_element_type=jnp.float32)
        behind = (z > 0) if to_right else (z < n - 1)

        @pl.when(behind)
        def _():
            chunk_copy(q, to_right).wait_recv()
            got = (from_left if to_right else from_right)[q]
            send[q] = (acc[...] + got.astype(jnp.float32)).astype(jnp.bfloat16)

        @pl.when(jnp.logical_not(behind))
        def _():
            send[q] = acc[...].astype(jnp.bfloat16)

        @pl.when(i >= AHEAD)
        def _():
            chunk_copy(q + AHEAD if to_right else q - AHEAD, to_right).wait_send()

        chunk_copy(q, to_right).start()

    def base_steps(step):
        right = step - z
        left = step - (n - 1 - z)

        @pl.when((right >= 0) & (chunks - 1 - right >= first_right))
        def _():
            base_step(right, chunks - 1 - right, True)

        @pl.when((left >= 0) & (left < first_own))
        def _():
            base_step(left, left, False)

    def rank_partial():
        @pl.loop(1, n_serve)
        def _(k):
            adapter_wait(k, down_send, down_got, down_ssem, down_rsem)

        for j in range(segs):
            at = pl.ds(j * seg_len, seg_len)
            rank_own[:, at] = lax.dot_general(
                down_got[owner_of(j)],
                tok[at, :],
                (((1,), (1,)), ((), ())),
                preferred_element_type=jnp.float32,
            )

    def rank_hop(to_right):
        side = 0 if to_right else 1
        behind = (z > 0) if to_right else (z < n - 1)
        ahead = (z < n - 1) if to_right else (z > 0)

        @pl.when(behind)
        def _():
            rank_copy(to_right).wait_recv()

            @pl.when(ahead)
            def _():
                rank_send[side] = (
                    rank_own[...] + rank_got[side].astype(jnp.float32)
                ).astype(jnp.bfloat16)

        @pl.when(jnp.logical_not(behind))
        def _():
            rank_got[side] = jnp.zeros(rank_got.shape[1:], rank_got.dtype)

            @pl.when(ahead)
            def _():
                rank_send[side] = rank_own[...].astype(jnp.bfloat16)

        @pl.when(ahead)
        def _():
            rank_copy(to_right).start()

    last = steps + n - 2
    first_rank = min(RANK_STEP, last)

    def rank_step_of(distance):
        return jnp.minimum(first_rank + RANK_LAG * distance, last)

    @pl.loop(0, 2)
    def _(i):
        base_steps(i)

    load_up.wait()

    @pl.loop(1, n_serve)
    def _(k):
        peer = lax.rem(me + k, n_serve)
        up_send[peer] = up[row_for(peer)]
        adapter_copy(k, up_send, up_got, up_ssem, up_rsem).start()

    up_got[me] = up[row_for(me)]

    @pl.loop(2, last + 1)
    def _(i):
        base_steps(i)

        @pl.when(i == first_rank)
        def _():
            rank_partial()

        @pl.when(i == rank_step_of(z))
        def _():
            rank_hop(True)

        @pl.when(i == rank_step_of(n - 1 - z))
        def _():
            rank_hop(False)

    @pl.loop(1, n_serve)
    def _(k):
        adapter_wait(k, up_send, up_got, up_ssem, up_rsem)

    coords = (
        rank_own[...] + rank_got[0].astype(jnp.float32) + rank_got[1].astype(jnp.float32)
    ).astype(jnp.bfloat16)
    for c in range(per):
        load_w(first_own + c).wait()
        own[c] = jnp.dot(tok[...], w[first_own + c], preferred_element_type=jnp.float32)
        for j in range(segs):
            at = pl.ds(j * seg_len, seg_len)
            own[c, at, :] += low_rank_scale * lax.dot_general(
                coords[:, j * seg_len : (j + 1) * seg_len],
                up_got[owner_of(j), :, c * WIDTH : (c + 1) * WIDTH],
                (((0,), (0,)), ((), ())),
                preferred_element_type=jnp.float32,
            )

    def out_copy(c):
        return pltpu.make_async_copy(
            out.at[c], out_hbm.at[:, pl.ds(pl.multiple_of(c * WIDTH, WIDTH), WIDTH)], out_sem.at[c]
        )

    @pl.loop(0, per)
    def _(k):
        c = jnp.where(2 * z < n, per - 1 - k, k)
        q = first_own + c

        @pl.when(z > 0)
        def _():
            chunk_copy(q, True).wait_recv()
            own[c] += from_left[q].astype(jnp.float32)

        @pl.when(z < n - 1)
        def _():
            chunk_copy(q, False).wait_recv()
            own[c] += from_right[q].astype(jnp.float32)

        out[c] = own[c].astype(jnp.bfloat16)
        out_copy(c).start()

    @pl.loop(0, per)
    def _(c):
        out_copy(c).wait()

    @pl.loop(0, steps)
    def _(i):
        @pl.when((chunks - 1 - i >= first_right) & (chunks - 1 - i - AHEAD < first_right))
        def _():
            chunk_copy(chunks - 1 - i, True).wait_send()

        @pl.when((i < first_own) & (i + AHEAD >= first_own))
        def _():
            chunk_copy(i, False).wait_send()

    @pl.when(z < n - 1)
    def _():
        rank_copy(True).wait_send()

    @pl.when(z > 0)
    def _():
        rank_copy(False).wait_send()


def on_device(
    n,
    n_serve,
    tokens,
    base_weight,
    adapter_down,
    adapter_up,
    segment_adapter,
    owner_map,
    segment_blocks,
):
    rows, depth = tokens.shape
    columns = base_weight.shape[1]
    chunks = columns // WIDTH
    out_width = columns // n
    per = out_width // WIDTH
    stored, rank, _ = adapter_down.shape
    bf16, f32 = jnp.bfloat16, jnp.float32
    smem = pl.BlockSpec(memory_space=pltpu.SMEM)
    anywhere = pl.BlockSpec(memory_space=pl.ANY)
    dma = pltpu.SemaphoreType.DMA
    summed = pl.pallas_call(
        functools.partial(kernel, n, n_serve),
        out_shape=jax.ShapeDtypeStruct((rows, out_width), bf16),
        in_specs=[smem, smem, anywhere, anywhere, anywhere, anywhere],
        out_specs=anywhere,
        scratch_shapes=[
            pltpu.VMEM((rows, depth), bf16),
            pltpu.VMEM((chunks, depth, WIDTH), bf16),
            pltpu.VMEM((rows, WIDTH), f32),
            pltpu.VMEM((chunks, rows, WIDTH), bf16),
            pltpu.VMEM((chunks, rows, WIDTH), bf16),
            pltpu.VMEM((chunks, rows, WIDTH), bf16),
            pltpu.VMEM((per, rows, WIDTH), f32),
            pltpu.VMEM((per, rows, WIDTH), bf16),
            pltpu.VMEM((stored, rank, depth), bf16),
            pltpu.VMEM((stored, rank, out_width), bf16),
            pltpu.VMEM((n_serve, rank, depth), bf16),
            pltpu.VMEM((n_serve, rank, out_width), bf16),
            pltpu.VMEM((n_serve, rank, depth), bf16),
            pltpu.VMEM((n_serve, rank, out_width), bf16),
            pltpu.VMEM((rank, rows), f32),
            pltpu.VMEM((2, rank, rows), bf16),
            pltpu.VMEM((2, rank, rows), bf16),
            dma((3,)),
            dma((chunks,)),
            dma((per,)),
            dma((chunks,)),
            dma((chunks,)),
            dma((chunks,)),
            dma((n_serve,)),
            dma((n_serve,)),
            dma((n_serve,)),
            dma((n_serve,)),
            dma((2,)),
            dma((2,)),
        ],
        compiler_params=pltpu.CompilerParams(
            collective_id=0, has_side_effects=True, vmem_limit_bytes=56 * 2**20
        ),
        cost_estimate=pl.CostEstimate(
            flops=2 * rows * depth * columns,
            bytes_accessed=2 * (depth * columns + rows * depth + rows * out_width),
            transcendentals=0,
        ),
    )(segment_adapter, owner_map, tokens, base_weight, adapter_down, adapter_up)
    segments = segment_blocks.shape[0]
    live = jnp.arange(rows // segments, dtype=jnp.int32)[None, :] < segment_blocks[:, None] * BLOCK
    return jnp.where(live.reshape(-1)[:, None], summed, jnp.zeros((), bf16))


def solution(mesh):
    in_specs = (
        P(("groups", "serve"), "tensor"),
        P("tensor", None),
        P("serve", None, "tensor"),
        P("serve", None, "tensor"),
        P("groups"),
        P("groups"),
        P(("groups", "serve")),
    )
    out_specs = P(("groups", "serve"), "tensor")
    return jax.shard_map(
        functools.partial(on_device, mesh.shape["tensor"], mesh.shape["serve"]),
        mesh=mesh,
        in_specs=in_specs,
        out_specs=out_specs,
        check_vma=False,
    )
```

```python
import functools

import jax
import jax.numpy as jnp
from jax import lax
from jax.experimental import pallas as pl
from jax.experimental.pallas import tpu as pltpu
from jax.sharding import PartitionSpec as P

MESH = pl.DeviceIdType.MESH
BLOCK = 128
WIDTH = 256
RANK_STEP = 3
RANK_LAG = 4
AHEAD = 3

low_rank_scale = 0.5


def kernel(
    n,
    n_serve,
    seg_adapter,
    owner_map,
    seg_blocks,
    tok_hbm,
    w_hbm,
    down_hbm,
    up_hbm,
    out,
    tok,
    w,
    acc,
    send,
    from_left,
    from_right,
    own,
    down,
    up,
    down_send,
    up_send,
    down_got,
    up_got,
    rank_own,
    rank_send,
    rank_got,
    local_sem,
    w_sem,
    send_sem,
    left_sem,
    right_sem,
    down_ssem,
    down_rsem,
    up_ssem,
    up_rsem,
    rank_ssem,
    rank_rsem,
):
    z = lax.axis_index("tensor")
    me = lax.axis_index("serve")
    chunks = w.shape[0]
    per = chunks // n
    steps = chunks - per
    stored, rank = down.shape[0], down.shape[1]
    rows = tok.shape[0]
    segs = seg_adapter.shape[0] // n_serve
    seg_len = rows // segs
    first_right = (z + 1) * per
    first_own = z * per

    def load_w(q):
        return pltpu.make_async_copy(
            w_hbm.at[:, pl.ds(pl.multiple_of(q * WIDTH, WIDTH), WIDTH)], w.at[q], w_sem.at[q]
        )

    load_tok = pltpu.make_async_copy(tok_hbm, tok, local_sem.at[0])
    load_down = pltpu.make_async_copy(down_hbm, down, local_sem.at[1])
    load_up = pltpu.make_async_copy(up_hbm, up, local_sem.at[2])

    barrier = pltpu.get_barrier_semaphore()

    @pl.loop(1, n_serve)
    def _(k):
        pl.semaphore_signal(
            barrier, inc=1, device_id={"serve": lax.rem(me + k, n_serve)}, device_id_type=MESH
        )

    @pl.when(z > 0)
    def _():
        pl.semaphore_signal(barrier, inc=1, device_id={"tensor": z - 1}, device_id_type=MESH)

    @pl.when(z < n - 1)
    def _():
        pl.semaphore_signal(barrier, inc=1, device_id={"tensor": z + 1}, device_id_type=MESH)

    load_tok.start()

    def load_step(i):
        @pl.when(chunks - 1 - i >= first_right)
        def _():
            load_w(chunks - 1 - i).start()

        @pl.when(i < first_own)
        def _():
            load_w(i).start()

    load_step(0)
    load_down.start()
    load_up.start()

    @pl.loop(1, steps)
    def _(i):
        load_step(i)

    @pl.loop(0, per)
    def _(c):
        load_w(first_own + c).start()

    def row_for(peer):
        row = jnp.int32(0)
        for j in range(segs):
            stored_row = owner_map[seg_adapter[peer * segs + j]]
            row += jnp.where(lax.div(stored_row, stored) == me, lax.rem(stored_row, stored), 0)
        return row

    def owner_of(j):
        return lax.div(owner_map[seg_adapter[me * segs + j]], stored)

    def adapter_copy(k, src, dst, ssem, rsem):
        peer = lax.rem(me + k, n_serve)
        return pltpu.make_async_remote_copy(
            src_ref=src.at[peer],
            dst_ref=dst.at[me],
            send_sem=ssem.at[peer],
            recv_sem=rsem.at[me],
            device_id={"serve": peer},
            device_id_type=MESH,
        )

    def adapter_wait(k, src, dst, ssem, rsem):
        peer = lax.rem(me + k, n_serve)
        got = pltpu.make_async_remote_copy(
            src_ref=src.at[peer],
            dst_ref=dst.at[peer],
            send_sem=ssem.at[peer],
            recv_sem=rsem.at[peer],
            device_id={"serve": peer},
            device_id_type=MESH,
        )
        got.wait_send()
        got.wait_recv()

    def product(q):
        load_w(q).wait()
        return jnp.dot(tok[...], w[q], preferred_element_type=jnp.float32)

    load_tok.wait()

    @pl.when(z == 0)
    def _():
        send[chunks - 1] = product(chunks - 1).astype(jnp.bfloat16)

    @pl.when(z == n - 1)
    def _():
        send[0] = product(0).astype(jnp.bfloat16)

    neighbours = (z > 0).astype(jnp.int32) + (z < n - 1).astype(jnp.int32)
    pl.semaphore_wait(barrier, n_serve - 1 + neighbours)

    def chunk_copy(q, to_right):
        return pltpu.make_async_remote_copy(
            src_ref=send.at[q],
            dst_ref=(from_left if to_right else from_right).at[q],
            send_sem=send_sem.at[q],
            recv_sem=(left_sem if to_right else right_sem).at[q],
            device_id={"tensor": z + 1 if to_right else z - 1},
            device_id_type=MESH,
        )

    def rank_copy(to_right):
        side = 0 if to_right else 1
        return pltpu.make_async_remote_copy(
            src_ref=rank_send.at[side],
            dst_ref=rank_got.at[side],
            send_sem=rank_ssem.at[side],
            recv_sem=rank_rsem.at[side],
            device_id={"tensor": z + 1 if to_right else z - 1},
            device_id_type=MESH,
        )

    @pl.when(z == 0)
    def _():
        chunk_copy(chunks - 1, True).start()

    @pl.when(z == n - 1)
    def _():
        chunk_copy(0, False).start()

    load_down.wait()

    @pl.loop(1, n_serve)
    def _(k):
        peer = lax.rem(me + k, n_serve)
        down_send[peer] = down[row_for(peer)]
        adapter_copy(k, down_send, down_got, down_ssem, down_rsem).start()

    down_got[me] = down[row_for(me)]
    def base_step(i, q, to_right):
        acc[...] = product(q)
        behind = (z > 0) if to_right else (z < n - 1)

        @pl.when(behind)
        def _():
            chunk_copy(q, to_right).wait_recv()
            got = (from_left if to_right else from_right)[q]
            send[q] = (acc[...] + got.astype(jnp.float32)).astype(jnp.bfloat16)

        @pl.when(jnp.logical_not(behind))
        def _():
            send[q] = acc[...].astype(jnp.bfloat16)

        @pl.when(i >= AHEAD)
        def _():
            chunk_copy(q + AHEAD if to_right else q - AHEAD, to_right).wait_send()

        chunk_copy(q, to_right).start()

    def base_steps(step):
        right = step - z
        left = step - (n - 1 - z)

        @pl.when((right >= 0) & (chunks - 1 - right >= first_right))
        def _():
            base_step(right, chunks - 1 - right, True)

        @pl.when((left >= 0) & (left < first_own))
        def _():
            base_step(left, left, False)

    def rank_partial():
        @pl.loop(1, n_serve)
        def _(k):
            adapter_wait(k, down_send, down_got, down_ssem, down_rsem)

        for j in range(segs):
            at = pl.ds(j * seg_len, seg_len)
            rank_own[:, at] = lax.dot_general(
                down_got[owner_of(j)],
                tok[at, :],
                (((1,), (1,)), ((), ())),
                preferred_element_type=jnp.float32,
            )

    def rank_hop(to_right):
        side = 0 if to_right else 1
        behind = (z > 0) if to_right else (z < n - 1)
        ahead = (z < n - 1) if to_right else (z > 0)

        @pl.when(behind)
        def _():
            rank_copy(to_right).wait_recv()

            @pl.when(ahead)
            def _():
                rank_send[side] = (
                    rank_own[...] + rank_got[side].astype(jnp.float32)
                ).astype(jnp.bfloat16)

        @pl.when(jnp.logical_not(behind))
        def _():
            rank_got[side] = jnp.zeros(rank_got.shape[1:], rank_got.dtype)

            @pl.when(ahead)
            def _():
                rank_send[side] = rank_own[...].astype(jnp.bfloat16)

        @pl.when(ahead)
        def _():
            rank_copy(to_right).start()

    last = steps + n - 2
    first_rank = min(RANK_STEP, last)

    def rank_step_of(distance):
        return jnp.minimum(first_rank + RANK_LAG * distance, last)

    base_steps(1)

    load_up.wait()

    @pl.loop(1, n_serve)
    def _(k):
        peer = lax.rem(me + k, n_serve)
        up_send[peer] = up[row_for(peer)]
        adapter_copy(k, up_send, up_got, up_ssem, up_rsem).start()

    up_got[me] = up[row_for(me)]

    @pl.loop(2, last + 1)
    def _(i):
        base_steps(i)

        @pl.when(i == first_rank)
        def _():
            rank_partial()

        @pl.when(i == rank_step_of(z))
        def _():
            rank_hop(True)

        @pl.when(i == rank_step_of(n - 1 - z))
        def _():
            rank_hop(False)

    @pl.loop(1, n_serve)
    def _(k):
        adapter_wait(k, up_send, up_got, up_ssem, up_rsem)

    coords = (
        rank_own[...] + rank_got[0].astype(jnp.float32) + rank_got[1].astype(jnp.float32)
    ).astype(jnp.bfloat16)
    for c in range(per):
        own[c] = product(first_own + c)
        for j in range(segs):
            at = pl.ds(j * seg_len, seg_len)
            own[c, at, :] += low_rank_scale * lax.dot_general(
                coords[:, j * seg_len : (j + 1) * seg_len],
                up_got[owner_of(j), :, c * WIDTH : (c + 1) * WIDTH],
                (((0,), (0,)), ((), ())),
                preferred_element_type=jnp.float32,
            )

    def finish(c, got):
        for j in range(segs):
            at = pl.ds(j * seg_len, seg_len)
            total = own[c, at, :] + got[first_own + c, at, :].astype(jnp.float32)
            row = lax.broadcasted_iota(jnp.int32, total.shape, 0)
            total = jnp.where(row < seg_blocks[j] * BLOCK, total, 0.0)
            out[at, pl.ds(pl.multiple_of(c * WIDTH, WIDTH), WIDTH)] = total.astype(jnp.bfloat16)

    @pl.when(2 * z < n)
    def _():
        @pl.loop(0, per)
        def _(k):
            c = per - 1 - k
            chunk_copy(first_own + c, False).wait_recv()

            @pl.when(z > 0)
            def _():
                own[c] += from_right[first_own + c].astype(jnp.float32)
                chunk_copy(first_own + c, True).wait_recv()
                finish(c, from_left)

            @pl.when(z == 0)
            def _():
                finish(c, from_right)

    @pl.when(2 * z >= n)
    def _():
        @pl.loop(0, per)
        def _(c):
            chunk_copy(first_own + c, True).wait_recv()

            @pl.when(z < n - 1)
            def _():
                own[c] += from_left[first_own + c].astype(jnp.float32)
                chunk_copy(first_own + c, False).wait_recv()
                finish(c, from_right)

            @pl.when(z == n - 1)
            def _():
                finish(c, from_left)

    @pl.loop(0, steps)
    def _(i):
        @pl.when((chunks - 1 - i >= first_right) & (chunks - 1 - i - AHEAD < first_right))
        def _():
            chunk_copy(chunks - 1 - i, True).wait_send()

        @pl.when((i < first_own) & (i + AHEAD >= first_own))
        def _():
            chunk_copy(i, False).wait_send()

    @pl.when(z < n - 1)
    def _():
        rank_copy(True).wait_send()

    @pl.when(z > 0)
    def _():
        rank_copy(False).wait_send()


def on_device(
    n,
    n_serve,
    tokens,
    base_weight,
    adapter_down,
    adapter_up,
    segment_adapter,
    owner_map,
    segment_blocks,
):
    rows, depth = tokens.shape
    columns = base_weight.shape[1]
    chunks = columns // WIDTH
    out_width = columns // n
    per = out_width // WIDTH
    stored, rank, _ = adapter_down.shape
    bf16, f32 = jnp.bfloat16, jnp.float32
    smem = pl.BlockSpec(memory_space=pltpu.SMEM)
    anywhere = pl.BlockSpec(memory_space=pl.ANY)
    dma = pltpu.SemaphoreType.DMA
    return pl.pallas_call(
        functools.partial(kernel, n, n_serve),
        out_shape=pltpu.VMEM((rows, out_width), bf16),
        in_specs=[smem, smem, smem, anywhere, anywhere, anywhere, anywhere],
        out_specs=pl.BlockSpec(memory_space=pltpu.VMEM),
        scratch_shapes=[
            pltpu.VMEM((rows, depth), bf16),
            pltpu.VMEM((chunks, depth, WIDTH), bf16),
            pltpu.VMEM((rows, WIDTH), f32),
            pltpu.VMEM((chunks, rows, WIDTH), bf16),
            pltpu.VMEM((chunks, rows, WIDTH), bf16),
            pltpu.VMEM((chunks, rows, WIDTH), bf16),
            pltpu.VMEM((per, rows, WIDTH), f32),
            pltpu.VMEM((stored, rank, depth), bf16),
            pltpu.VMEM((stored, rank, out_width), bf16),
            pltpu.VMEM((n_serve, rank, depth), bf16),
            pltpu.VMEM((n_serve, rank, out_width), bf16),
            pltpu.VMEM((n_serve, rank, depth), bf16),
            pltpu.VMEM((n_serve, rank, out_width), bf16),
            pltpu.VMEM((rank, rows), f32),
            pltpu.VMEM((2, rank, rows), bf16),
            pltpu.VMEM((2, rank, rows), bf16),
            dma((3,)),
            dma((chunks,)),
            dma((chunks,)),
            dma((chunks,)),
            dma((chunks,)),
            dma((n_serve,)),
            dma((n_serve,)),
            dma((n_serve,)),
            dma((n_serve,)),
            dma((2,)),
            dma((2,)),
        ],
        compiler_params=pltpu.CompilerParams(
            collective_id=0, has_side_effects=True, vmem_limit_bytes=56 * 2**20
        ),
        cost_estimate=pl.CostEstimate(
            flops=2 * rows * depth * columns,
            bytes_accessed=2 * (depth * columns + rows * depth + rows * out_width),
            transcendentals=0,
        ),
    )(
        segment_adapter,
        owner_map,
        segment_blocks,
        tokens,
        base_weight,
        adapter_down,
        adapter_up,
    )


def solution(mesh):
    in_specs = (
        P(("groups", "serve"), "tensor"),
        P("tensor", None),
        P("serve", None, "tensor"),
        P("serve", None, "tensor"),
        P("groups"),
        P("groups"),
        P(("groups", "serve")),
    )
    out_specs = P(("groups", "serve"), "tensor")
    return jax.shard_map(
        functools.partial(on_device, mesh.shape["tensor"], mesh.shape["serve"]),
        mesh=mesh,
        in_specs=in_specs,
        out_specs=out_specs,
        check_vma=False,
    )
```

```python
import functools

import jax
import jax.numpy as jnp
from jax import lax
from jax.experimental import pallas as pl
from jax.experimental.pallas import tpu as pltpu
from jax.sharding import PartitionSpec as P

MESH = pl.DeviceIdType.MESH
BLOCK = 128
WIDTH = 256
RANK_STEP = 3
RANK_LAG = 4
AHEAD = 3

low_rank_scale = 0.5


def kernel(
    n,
    n_serve,
    seg_adapter,
    owner_map,
    seg_blocks,
    tok_hbm,
    w_hbm,
    down_hbm,
    up_hbm,
    out,
    tok,
    w,
    acc,
    send,
    from_left,
    from_right,
    own,
    down,
    up,
    down_send,
    up_send,
    down_got,
    up_got,
    rank_own,
    rank_send,
    rank_got,
    local_sem,
    w_sem,
    send_sem,
    left_sem,
    right_sem,
    down_ssem,
    down_rsem,
    up_ssem,
    up_rsem,
    rank_ssem,
    rank_rsem,
):
    z = lax.axis_index("tensor")
    me = lax.axis_index("serve")
    chunks = w.shape[0]
    per = chunks // n
    steps = chunks - per
    stored, rank = down.shape[0], down.shape[1]
    rows = tok.shape[0]
    segs = seg_adapter.shape[0] // n_serve
    seg_len = rows // segs
    first_right = (z + 1) * per
    first_own = z * per

    def load_w(q):
        return pltpu.make_async_copy(
            w_hbm.at[:, pl.ds(pl.multiple_of(q * WIDTH, WIDTH), WIDTH)], w.at[q], w_sem.at[q]
        )

    half = rows // 2

    def load_tok(h):
        at = pl.ds(h * half, half)
        return pltpu.make_async_copy(tok_hbm.at[at, :], tok.at[at, :], local_sem.at[3 * h])

    load_down = pltpu.make_async_copy(down_hbm, down, local_sem.at[1])
    load_up = pltpu.make_async_copy(up_hbm, up, local_sem.at[2])

    def load_step(i):
        @pl.when(chunks - 1 - i >= first_right)
        def _():
            load_w(chunks - 1 - i).start()

        @pl.when(i < first_own)
        def _():
            load_w(i).start()

    load_tok(0).start()
    load_step(0)
    load_tok(1).start()
    barrier = pltpu.get_barrier_semaphore()

    @pl.loop(1, n_serve)
    def _(k):
        pl.semaphore_signal(
            barrier, inc=1, device_id={"serve": lax.rem(me + k, n_serve)}, device_id_type=MESH
        )

    @pl.when(z > 0)
    def _():
        pl.semaphore_signal(barrier, inc=1, device_id={"tensor": z - 1}, device_id_type=MESH)

    @pl.when(z < n - 1)
    def _():
        pl.semaphore_signal(barrier, inc=1, device_id={"tensor": z + 1}, device_id_type=MESH)

    def row_for(peer):
        row = jnp.int32(0)
        for j in range(segs):
            stored_row = owner_map[seg_adapter[peer * segs + j]]
            row += jnp.where(lax.div(stored_row, stored) == me, lax.rem(stored_row, stored), 0)
        return row

    def owner_of(j):
        return lax.div(owner_map[seg_adapter[me * segs + j]], stored)

    def adapter_copy(k, src, dst, ssem, rsem):
        peer = lax.rem(me + k, n_serve)
        return pltpu.make_async_remote_copy(
            src_ref=src.at[peer],
            dst_ref=dst.at[me],
            send_sem=ssem.at[peer],
            recv_sem=rsem.at[me],
            device_id={"serve": peer},
            device_id_type=MESH,
        )

    def adapter_wait(k, src, dst, ssem, rsem):
        peer = lax.rem(me + k, n_serve)
        got = pltpu.make_async_remote_copy(
            src_ref=src.at[peer],
            dst_ref=dst.at[peer],
            send_sem=ssem.at[peer],
            recv_sem=rsem.at[peer],
            device_id={"serve": peer},
            device_id_type=MESH,
        )
        got.wait_send()
        got.wait_recv()

    def product(q):
        load_w(q).wait()
        return jnp.dot(tok[...], w[q], preferred_element_type=jnp.float32)

    def first_half(q, h):
        at = pl.ds(h * half, half)
        send[q, at, :] = jnp.dot(tok[at, :], w[q], preferred_element_type=jnp.float32).astype(
            jnp.bfloat16
        )

    load_tok(0).wait()

    @pl.when(z == 0)
    def _():
        load_w(chunks - 1).wait()
        first_half(chunks - 1, 0)

    @pl.when(z == n - 1)
    def _():
        load_w(0).wait()
        first_half(0, 0)

    load_down.start()
    load_up.start()

    @pl.loop(1, steps)
    def _(i):
        load_step(i)

    @pl.loop(0, per)
    def _(c):
        load_w(first_own + c).start()

    neighbours = (z > 0).astype(jnp.int32) + (z < n - 1).astype(jnp.int32)
    pl.semaphore_wait(barrier, n_serve - 1 + neighbours)

    def chunk_copy(q, to_right):
        return pltpu.make_async_remote_copy(
            src_ref=send.at[q],
            dst_ref=(from_left if to_right else from_right).at[q],
            send_sem=send_sem.at[q],
            recv_sem=(left_sem if to_right else right_sem).at[q],
            device_id={"tensor": z + 1 if to_right else z - 1},
            device_id_type=MESH,
        )

    def rank_copy(to_right):
        side = 0 if to_right else 1
        return pltpu.make_async_remote_copy(
            src_ref=rank_send.at[side],
            dst_ref=rank_got.at[side],
            send_sem=rank_ssem.at[side],
            recv_sem=rank_rsem.at[side],
            device_id={"tensor": z + 1 if to_right else z - 1},
            device_id_type=MESH,
        )

    def half_copy(q, h, to_right):
        at = pl.ds(h * half, half)
        return pltpu.make_async_remote_copy(
            src_ref=send.at[q, at, :],
            dst_ref=(from_left if to_right else from_right).at[q, at, :],
            send_sem=send_sem.at[q],
            recv_sem=(left_sem if to_right else right_sem).at[q],
            device_id={"tensor": z + 1 if to_right else z - 1},
            device_id_type=MESH,
        )

    @pl.when(z == 0)
    def _():
        half_copy(chunks - 1, 0, True).start()

    @pl.when(z == n - 1)
    def _():
        half_copy(0, 0, False).start()

    load_tok(1).wait()

    @pl.when(z == 0)
    def _():
        first_half(chunks - 1, 1)
        half_copy(chunks - 1, 1, True).start()

    @pl.when(z == n - 1)
    def _():
        first_half(0, 1)
        half_copy(0, 1, False).start()

    load_down.wait()

    @pl.loop(1, n_serve)
    def _(k):
        peer = lax.rem(me + k, n_serve)
        down_send[peer] = down[row_for(peer)]
        adapter_copy(k, down_send, down_got, down_ssem, down_rsem).start()

    down_got[me] = down[row_for(me)]
    def base_step(i, q, to_right):
        acc[...] = product(q)
        behind = (z > 0) if to_right else (z < n - 1)

        @pl.when(behind)
        def _():
            chunk_copy(q, to_right).wait_recv()
            got = (from_left if to_right else from_right)[q]
            send[q] = (acc[...] + got.astype(jnp.float32)).astype(jnp.bfloat16)

        @pl.when(jnp.logical_not(behind))
        def _():
            send[q] = acc[...].astype(jnp.bfloat16)

        @pl.when(i >= AHEAD)
        def _():
            chunk_copy(q + AHEAD if to_right else q - AHEAD, to_right).wait_send()

        chunk_copy(q, to_right).start()

    def base_steps(step):
        right = step - z
        left = step - (n - 1 - z)

        @pl.when((right >= 0) & (chunks - 1 - right >= first_right))
        def _():
            base_step(right, chunks - 1 - right, True)

        @pl.when((left >= 0) & (left < first_own))
        def _():
            base_step(left, left, False)

    def rank_partial():
        @pl.loop(1, n_serve)
        def _(k):
            adapter_wait(k, down_send, down_got, down_ssem, down_rsem)

        for j in range(segs):
            at = pl.ds(j * seg_len, seg_len)
            rank_own[:, at] = lax.dot_general(
                down_got[owner_of(j)],
                tok[at, :],
                (((1,), (1,)), ((), ())),
                preferred_element_type=jnp.float32,
            )

    def rank_hop(to_right):
        side = 0 if to_right else 1
        behind = (z > 0) if to_right else (z < n - 1)
        ahead = (z < n - 1) if to_right else (z > 0)

        @pl.when(behind)
        def _():
            rank_copy(to_right).wait_recv()

            @pl.when(ahead)
            def _():
                rank_send[side] = (
                    rank_own[...] + rank_got[side].astype(jnp.float32)
                ).astype(jnp.bfloat16)

        @pl.when(jnp.logical_not(behind))
        def _():
            rank_got[side] = jnp.zeros(rank_got.shape[1:], rank_got.dtype)

            @pl.when(ahead)
            def _():
                rank_send[side] = rank_own[...].astype(jnp.bfloat16)

        @pl.when(ahead)
        def _():
            rank_copy(to_right).start()

    last = steps + n - 2
    first_rank = min(RANK_STEP, last)

    def rank_step_of(distance):
        return jnp.minimum(first_rank + RANK_LAG * distance, last)

    base_steps(1)

    load_up.wait()

    @pl.loop(1, n_serve)
    def _(k):
        peer = lax.rem(me + k, n_serve)
        up_send[peer] = up[row_for(peer)]
        adapter_copy(k, up_send, up_got, up_ssem, up_rsem).start()

    up_got[me] = up[row_for(me)]

    @pl.loop(2, last + 1)
    def _(i):
        base_steps(i)

        @pl.when(i == first_rank)
        def _():
            rank_partial()

        @pl.when(i == rank_step_of(z))
        def _():
            rank_hop(True)

        @pl.when(i == rank_step_of(n - 1 - z))
        def _():
            rank_hop(False)

    @pl.loop(1, n_serve)
    def _(k):
        adapter_wait(k, up_send, up_got, up_ssem, up_rsem)

    coords = (
        rank_own[...] + rank_got[0].astype(jnp.float32) + rank_got[1].astype(jnp.float32)
    ).astype(jnp.bfloat16)
    for c in range(per):
        own[c] = product(first_own + c)
        for j in range(segs):
            at = pl.ds(j * seg_len, seg_len)
            own[c, at, :] += low_rank_scale * lax.dot_general(
                coords[:, j * seg_len : (j + 1) * seg_len],
                up_got[owner_of(j), :, c * WIDTH : (c + 1) * WIDTH],
                (((0,), (0,)), ((), ())),
                preferred_element_type=jnp.float32,
            )

    def finish(c, got):
        for j in range(segs):
            at = pl.ds(j * seg_len, seg_len)
            total = own[c, at, :] + got[first_own + c, at, :].astype(jnp.float32)
            row = lax.broadcasted_iota(jnp.int32, total.shape, 0)
            total = jnp.where(row < seg_blocks[j] * BLOCK, total, 0.0)
            out[at, pl.ds(pl.multiple_of(c * WIDTH, WIDTH), WIDTH)] = total.astype(jnp.bfloat16)

    @pl.when(2 * z < n)
    def _():
        @pl.loop(0, per)
        def _(k):
            c = per - 1 - k
            chunk_copy(first_own + c, False).wait_recv()

            @pl.when(z > 0)
            def _():
                own[c] += from_right[first_own + c].astype(jnp.float32)
                chunk_copy(first_own + c, True).wait_recv()
                finish(c, from_left)

            @pl.when(z == 0)
            def _():
                finish(c, from_right)

    @pl.when(2 * z >= n)
    def _():
        @pl.loop(0, per)
        def _(c):
            chunk_copy(first_own + c, True).wait_recv()

            @pl.when(z < n - 1)
            def _():
                own[c] += from_left[first_own + c].astype(jnp.float32)
                chunk_copy(first_own + c, False).wait_recv()
                finish(c, from_right)

            @pl.when(z == n - 1)
            def _():
                finish(c, from_left)

    @pl.loop(0, steps)
    def _(i):
        @pl.when((chunks - 1 - i >= first_right) & (chunks - 1 - i - AHEAD < first_right))
        def _():
            chunk_copy(chunks - 1 - i, True).wait_send()

        @pl.when((i < first_own) & (i + AHEAD >= first_own))
        def _():
            chunk_copy(i, False).wait_send()

    @pl.when(z < n - 1)
    def _():
        rank_copy(True).wait_send()

    @pl.when(z > 0)
    def _():
        rank_copy(False).wait_send()


def on_device(
    n,
    n_serve,
    tokens,
    base_weight,
    adapter_down,
    adapter_up,
    segment_adapter,
    owner_map,
    segment_blocks,
):
    rows, depth = tokens.shape
    columns = base_weight.shape[1]
    chunks = columns // WIDTH
    out_width = columns // n
    per = out_width // WIDTH
    stored, rank, _ = adapter_down.shape
    bf16, f32 = jnp.bfloat16, jnp.float32
    smem = pl.BlockSpec(memory_space=pltpu.SMEM)
    anywhere = pl.BlockSpec(memory_space=pl.ANY)
    dma = pltpu.SemaphoreType.DMA
    return pl.pallas_call(
        functools.partial(kernel, n, n_serve),
        out_shape=pltpu.VMEM((rows, out_width), bf16),
        in_specs=[smem, smem, smem, anywhere, anywhere, anywhere, anywhere],
        out_specs=pl.BlockSpec(memory_space=pltpu.VMEM),
        scratch_shapes=[
            pltpu.VMEM((rows, depth), bf16),
            pltpu.VMEM((chunks, depth, WIDTH), bf16),
            pltpu.VMEM((rows, WIDTH), f32),
            pltpu.VMEM((chunks, rows, WIDTH), bf16),
            pltpu.VMEM((chunks, rows, WIDTH), bf16),
            pltpu.VMEM((chunks, rows, WIDTH), bf16),
            pltpu.VMEM((per, rows, WIDTH), f32),
            pltpu.VMEM((stored, rank, depth), bf16),
            pltpu.VMEM((stored, rank, out_width), bf16),
            pltpu.VMEM((n_serve, rank, depth), bf16),
            pltpu.VMEM((n_serve, rank, out_width), bf16),
            pltpu.VMEM((n_serve, rank, depth), bf16),
            pltpu.VMEM((n_serve, rank, out_width), bf16),
            pltpu.VMEM((rank, rows), f32),
            pltpu.VMEM((2, rank, rows), bf16),
            pltpu.VMEM((2, rank, rows), bf16),
            dma((4,)),
            dma((chunks,)),
            dma((chunks,)),
            dma((chunks,)),
            dma((chunks,)),
            dma((n_serve,)),
            dma((n_serve,)),
            dma((n_serve,)),
            dma((n_serve,)),
            dma((2,)),
            dma((2,)),
        ],
        compiler_params=pltpu.CompilerParams(
            collective_id=0, has_side_effects=True, vmem_limit_bytes=56 * 2**20
        ),
        cost_estimate=pl.CostEstimate(
            flops=2 * rows * depth * columns,
            bytes_accessed=2 * (depth * columns + rows * depth + rows * out_width),
            transcendentals=0,
        ),
    )(
        segment_adapter,
        owner_map,
        segment_blocks,
        tokens,
        base_weight,
        adapter_down,
        adapter_up,
    )


def solution(mesh):
    in_specs = (
        P(("groups", "serve"), "tensor"),
        P("tensor", None),
        P("serve", None, "tensor"),
        P("serve", None, "tensor"),
        P("groups"),
        P("groups"),
        P(("groups", "serve")),
    )
    out_specs = P(("groups", "serve"), "tensor")
    return jax.shard_map(
        functools.partial(on_device, mesh.shape["tensor"], mesh.shape["serve"]),
        mesh=mesh,
        in_specs=in_specs,
        out_specs=out_specs,
        check_vma=False,
    )
```
